256 devices in a mesh: frame: 16 (over x_lo, y, core), head: 16 (over z, x_hi).
Axes of the slice: x: 4 (x_hi: 2, x_lo: 2; x = x_hi * 2 + x_lo), y: 4, z: 8, core: 2. Of those that a mesh axis runs over, the one named last changes fastest.
Arguments:
- video: bfloat16 [32768, 1536], P(('frame', 'head')), may hold values from -6 to 6
- audio_keys: bfloat16 [32768, 1536], P(('frame', 'head')), may hold values from -240 to 240
- audio_values: bfloat16 [32768, 1536], P(('frame', 'head')), may hold values from -6 to 6
- query_weight: bfloat16 [1536, 1536], P(('frame', 'head')), may hold values from -0.15625 to 0.15625
- d_out: bfloat16 [32768, 1536], P(('frame', 'head')), may hold values from -6 to 6
- win_start: int32 [256], P(('frame', 'head')), may hold values from 0 to 255
- win_count: int32 [256], P(('frame', 'head')), may hold values from 1 to 5, as said below
Outputs:
- attended: bfloat16 [32768, 1536], P(('frame', 'head'))
- grad_video: bfloat16 [32768, 1536], P(('frame', 'head'))
- grad_query_weight: float32 [1536, 1536], P(('frame', 'head'))
- grad_keys: float32 [32768, 1536], P(('frame', 'head'))
- grad_values: float32 [32768, 1536], P(('frame', 'head'))
The draws below stay inside these ranges and needn't reach their ends.
Inputs may be any that keep to these rules, and one draw needn't show every extreme that they name: `win_count`: each frame group's window lies within 2 blocks of the block with the same index as the group's device (group g on device g) and within the 256 blocks; some group has a window of 5 blocks.
All inputs are finite; a program needn't handle non-finite values.
Results may differ from the reference program's by a relative error of at most 0.04.
The reference program's roundings to bfloat16 on the way (of `queries`, `probs_half`, `score_grad` and `query_grad`) count: a program that leaves them out, or rounds other values in their place, can miss the bound.
Values may be sent and summed in bfloat16 or wider, within the bound.
A program may use at most 128 MiB of HBM per device.

```python
import math
import jax
import jax.numpy as jnp
from jax import lax

HEADS = 12
HEAD_DIM = 128
D = 1536
VT_DEV = 128
AT_DEV = 128
GROUP = 128
REACH = 2
NBLK = 256
GROUPS_DEV = 1
VTOK = 32768
ATOK = 32768


def window_table(key):
    group_total = NBLK * GROUPS_DEV
    group_ids = jnp.arange(group_total, dtype=jnp.int32)
    owner = group_ids // GROUPS_DEV
    lowest = jnp.maximum(owner - REACH, 0)
    highest = jnp.minimum(owner + REACH, NBLK - 1)
    spread = highest - lowest + 1
    count_key = jax.random.fold_in(key, 1)
    start_key = jax.random.fold_in(key, 2)
    counts = jax.random.randint(count_key, (group_total,), 1, 2 * REACH + 2)
    counts = jnp.minimum(counts, spread)
    slack = spread - counts
    starts = lowest + jax.random.randint(start_key, (group_total,), 0, slack + 1)
    chosen = group_ids == NBLK // 2 * GROUPS_DEV
    counts = jnp.where(chosen, spread, counts)
    starts = jnp.where(chosen, lowest, starts)
    return (starts.astype(jnp.int32), counts.astype(jnp.int32))


def draw_win_start(key, part):
    starts, counts = window_table(key)
    return starts


def draw_win_count(key, part):
    starts, counts = window_table(key)
    return counts


def draw_audio_keys(key, part):
    key = jax.random.fold_in(key, 7)
    base_key = jax.random.fold_in(key, 0)
    values_f = jnp.clip(jax.random.normal(base_key, (ATOK, D), jnp.float32), -5.0, 5.0)
    return values_f.astype(jnp.bfloat16)


def shard_levels(stream_key, dims, pieces, low, largest):
    def one(axis_at, shards_of):
        heights = jax.random.uniform(jax.random.fold_in(jax.random.fold_in(stream_key, 6), axis_at), (shards_of,), jnp.float32, low / len(pieces), largest / len(pieces))
        return jnp.repeat(jnp.exp(heights), dims[axis_at] // shards_of).reshape((-1,) + (1,) * (len(dims) - axis_at - 1))

    level = one(*pieces[0])
    for cut in pieces[1:]:
        level = level * one(*cut)
    return level


def noise(stream_key, dims, scale, reach, shards=(), kind=jnp.bfloat16):
    gain = shard_levels(stream_key, dims, shards, -0.22, 0.18) if shards else 1.0
    result = jax.random.normal(stream_key, dims, jnp.float32) * scale * gain
    return jnp.minimum(jnp.maximum(result, -reach), reach).astype(kind)


def setup_inputs(seed: int = 0) -> dict:
    key_of = jax.random.split(jax.random.key(seed), 8)
    return {
        "video": noise(key_of[0], (VTOK, D), 1.0, 6.0, ((0, 256),)),
        "audio_keys": draw_audio_keys(jax.random.fold_in(key_of[7], 71), 0),
        "audio_values": noise(key_of[2], (ATOK, D), 1.0, 6.0, ((0, 256),)),
        "query_weight": noise(key_of[3], (D, D), D ** -0.5, 0.15625, ((0, 256),)),
        "d_out": noise(key_of[4], (VTOK, D), 1.0, 6.0, ((0, 256),)),
        "win_start": draw_win_start(jax.random.fold_in(key_of[7], 71), 0),
        "win_count": draw_win_count(jax.random.fold_in(key_of[7], 71), 0),
    }


def attend(queries, key_rows, value_rows, grad_rows, allowed):
    row_count = queries.shape[0]
    length = key_rows.shape[0]
    scaling = 1.0 / math.sqrt(HEAD_DIM)
    query_heads = queries.astype(jnp.float32).reshape(row_count, HEADS, HEAD_DIM)
    key_heads = key_rows.astype(jnp.float32).reshape(length, HEADS, HEAD_DIM)
    value_heads = value_rows.astype(jnp.float32).reshape(length, HEADS, HEAD_DIM)
    grad_heads = grad_rows.astype(jnp.float32).reshape(row_count, HEADS, HEAD_DIM)
    scores = jnp.einsum('rhd,lhd->hrl', query_heads, key_heads) * scaling
    scores = jnp.where(allowed[None], scores, -1e+30)
    top_score = lax.optimization_barrier(jnp.max(scores, axis=-1, keepdims=True))
    exponent = jnp.exp(scores - top_score)
    probs_full = exponent / lax.optimization_barrier(jnp.sum(exponent, axis=-1, keepdims=True))
    probs_half = lax.optimization_barrier(probs_full.astype(jnp.bfloat16))
    attended = jnp.einsum('hrl,lhd->rhd', probs_half.astype(jnp.float32), value_heads)
    attended = attended.astype(jnp.bfloat16).reshape(row_count, HEADS * HEAD_DIM)
    prob_grad = jnp.einsum('rhd,lhd->hrl', grad_heads, value_heads)
    row_delta = lax.optimization_barrier(jnp.sum(probs_full * prob_grad, axis=-1, keepdims=True))
    score_grad = lax.optimization_barrier((probs_full * (prob_grad - row_delta) * scaling).astype(jnp.bfloat16))
    score_float = score_grad.astype(jnp.float32)
    query_grad = jnp.einsum('hrl,lhd->rhd', score_float, key_heads).astype(jnp.bfloat16)
    query_grad = query_grad.reshape(row_count, HEADS * HEAD_DIM)
    key_grad = jnp.einsum('hrl,rhd->lhd', score_float, query_heads).reshape(length, HEADS * HEAD_DIM)
    value_grad = jnp.einsum('hrl,rhd->lhd', probs_half.astype(jnp.float32), grad_heads).reshape(length, HEADS * HEAD_DIM)
    return (attended, query_grad, key_grad, value_grad)

def reference(video, audio_keys, audio_values, query_weight, d_out, win_start, win_count):
    queries = jnp.dot(video, query_weight, preferred_element_type=jnp.float32).astype(jnp.bfloat16)
    padding = jnp.zeros((REACH * AT_DEV, D), jnp.bfloat16)
    key_pad = jnp.concatenate([padding, audio_keys, padding], axis=0)
    value_pad = jnp.concatenate([padding, audio_values, padding], axis=0)
    length = (2 * REACH + 1) * AT_DEV
    pad_rows = ATOK + 2 * REACH * AT_DEV

    def one_block(running, block_index):
        key_acc, value_acc = running
        query_rows = lax.dynamic_slice_in_dim(queries, block_index * VT_DEV, VT_DEV)
        grad_rows = lax.dynamic_slice_in_dim(d_out, block_index * VT_DEV, VT_DEV)
        key_rows = lax.dynamic_slice_in_dim(key_pad, block_index * AT_DEV, length)
        value_rows = lax.dynamic_slice_in_dim(value_pad, block_index * AT_DEV, length)
        starts = lax.dynamic_slice_in_dim(win_start, block_index * GROUPS_DEV, GROUPS_DEV)
        counts = lax.dynamic_slice_in_dim(win_count, block_index * GROUPS_DEV, GROUPS_DEV)
        row_start = jnp.repeat(starts, GROUP, total_repeat_length=VT_DEV)
        row_end = row_start + jnp.repeat(counts, GROUP, total_repeat_length=VT_DEV)
        key_block = block_index - REACH + jnp.arange(length, dtype=jnp.int32) // AT_DEV
        allowed = (key_block[None, :] >= row_start[:, None]) & (key_block[None, :] < row_end[:, None])
        attended, query_grad, key_grad, value_grad = attend(query_rows, key_rows, value_rows, grad_rows, allowed)
        key_old = lax.dynamic_slice_in_dim(key_acc, block_index * AT_DEV, length)
        value_old = lax.dynamic_slice_in_dim(value_acc, block_index * AT_DEV, length)
        key_acc = lax.dynamic_update_slice_in_dim(key_acc, key_old + key_grad, block_index * AT_DEV, 0)
        value_acc = lax.dynamic_update_slice_in_dim(value_acc, value_old + value_grad, block_index * AT_DEV, 0)
        return ((key_acc, value_acc), (attended, query_grad))
    start_acc = (jnp.zeros((pad_rows, D), jnp.float32), jnp.zeros((pad_rows, D), jnp.float32))
    (key_acc, value_acc), (attended, query_grad) = lax.scan(one_block, start_acc, jnp.arange(NBLK, dtype=jnp.int32))
    attended = attended.reshape(VTOK, D)
    query_grad = query_grad.reshape(VTOK, D)
    grad_video = jnp.dot(query_grad, query_weight.T, preferred_element_type=jnp.float32).astype(jnp.bfloat16)
    grad_query_weight = jnp.dot(video.T, query_grad, preferred_element_type=jnp.float32)
    grad_keys = key_acc[REACH * AT_DEV:REACH * AT_DEV + ATOK]
    grad_values = value_acc[REACH * AT_DEV:REACH * AT_DEV + ATOK]
    return (attended, grad_video, grad_query_weight, grad_keys, grad_values)
```

```python
import math

import jax
import jax.numpy as jnp
from jax import lax
from jax.experimental import pallas as pl
from jax.experimental.pallas import tpu as pltpu
from jax.sharding import PartitionSpec as P

MESH = pl.DeviceIdType.MESH
HD = 128
D = 1536
HALF = 768
ROWS = 128
NG = 3
GW = HALF // NG
FR = 96
SCALE = 1.0 / math.sqrt(HD)
F32 = jnp.float32
BF16 = jnp.bfloat16
NSEM = 128


def dot(a, b, ca, cb):
    return lax.dot_general(a, b, (((ca,), (cb,)), ((), ())), preferred_element_type=F32)


def kernel(
    ws_ref, wc_ref, video, keys, values, d_out, w_ref,
    att_out, gvid_out, wg_out, gk_out, gv_out,
    ssem, rsem, lsem,
    win, wf, w_send, w_small, w_full, w_tmp,
    vid, vid_t, k_buf, v_buf, do_buf, q_buf, mask, att_buf, qg_buf,
    gh_send, gh_recv, g_mid, x_send, x_recv, gv_send, gv_recv, gv_own,
    wgp, e_recv, d_own, d_send, d_recv, c_part, c_recv, b_tmp, b_part, b_recv, a_part, a_recv,
):
    f = lax.axis_index("frame")
    h = lax.axis_index("head")
    s = lax.rem(h, 2)
    z = h // 2
    x_lo = f // 8
    y = lax.rem(f // 2, 4)
    core = lax.rem(f, 2)
    p = f * 16 + h

    partner = (f, z * 2 + 1 - s)

    def z_dev(d):
        return (f, lax.rem(z + d, 8) * 2 + s)

    def y_of(d):
        return lax.rem(y + d, 4)

    def y_dev(d):
        return (x_lo * 8 + y_of(d) * 2 + core, h)

    xlo_dev = ((1 - x_lo) * 8 + y * 2 + core, h)
    core_dev = (x_lo * 8 + y * 2 + 1 - core, h)

    def halo_dev(d):
        q = lax.rem(p + d + 256, 256)
        return (q // 16, lax.rem(q, 16))

    def mine(g):
        return pl.ds(pl.multiple_of(s * HALF + g * GW, 128), GW)

    def theirs(g):
        return pl.ds(pl.multiple_of((1 - s) * HALF + g * GW, 128), GW)

    count = [0]
    sent = []

    def remote(src, dst, dev):
        i = count[0]
        count[0] += 1
        cp = pltpu.make_async_remote_copy(
            src_ref=src, dst_ref=dst, send_sem=ssem.at[i], recv_sem=rsem.at[i],
            device_id=dev, device_id_type=MESH,
        )
        sent.append(cp)
        return cp

    local = [
        pltpu.make_async_copy(video, vid.at[0:ROWS], lsem.at[0]),
        pltpu.make_async_copy(keys.at[:, pl.ds(pl.multiple_of(s * HALF, 128), HALF)], k_buf.at[256:384], lsem.at[1]),
        pltpu.make_async_copy(values.at[:, pl.ds(pl.multiple_of(s * HALF, 128), HALF)], v_buf.at[256:384], lsem.at[2]),
        pltpu.make_async_copy(d_out.at[:, pl.ds(pl.multiple_of(s * HALF, 128), HALF)], do_buf.at[0:ROWS], lsem.at[3]),
    ]
    for cp in local:
        cp.start()

    barrier = pltpu.get_barrier_semaphore()
    peers = [partner] + [z_dev(d) for d in range(1, 8)] + [y_dev(d) for d in range(1, 4)]
    peers += [xlo_dev, core_dev, halo_dev(-2), halo_dev(2)]
    for dev in peers:
        pl.semaphore_signal(barrier, inc=1, device_id=dev, device_id_type=MESH)

    win[0, 0] = jnp.full((8, 128), ws_ref[0], jnp.int32)
    win[0, 1] = jnp.full((8, 128), ws_ref[0] + wc_ref[0], jnp.int32)
    wf[...] = jnp.zeros_like(wf)
    wf[0:6, :] = w_ref[...].astype(F32)
    for k in range(2):
        for ct in range(0, 6, 2):
            col = k * HALF + ct * 128
            pair = jnp.concatenate([wf[:, col : col + 128], wf[:, col + 128 : col + 256]], axis=0)
            w_send[k, ct * 8 : ct * 8 + 16, :] = pair.astype(BF16)

    pl.semaphore_wait(barrier, len(peers))

    wa = remote(w_send.at[1 - s], w_small.at[h], partner)
    wa.start()
    wl = pltpu.make_async_copy(w_send.at[s], w_small.at[h], lsem.at[4])
    wl.start()
    win_cp = remote(win.at[0], win.at[1], partner)
    win_cp.start()
    kx, vx, dx = [], [], []
    for g in range(NG):
        c = pl.ds(g * GW, GW)
        kx.append(remote(keys.at[:, theirs(g)], k_buf.at[384:512, c], partner))
        vx.append(remote(values.at[:, theirs(g)], v_buf.at[384:512, c], partner))
        kx[g].start()
        vx[g].start()
    vid_cp = remote(video, vid.at[ROWS : 2 * ROWS], partner)
    vid_cp.start()
    for g in range(NG):
        c = pl.ds(g * GW, GW)
        dx.append(remote(d_out.at[:, theirs(g)], do_buf.at[ROWS : 2 * ROWS, c], partner))
        dx[g].start()

    wl.wait()
    wa.wait_recv()
    zb = []
    for d in range(1, 8):
        pair = w_small.at[pl.ds(z * 2, 2)]
        zb.append(remote(pair, pair, z_dev(d)))
        zb[-1].start()

    halo_own = []
    for g in range(NG):
        c = pl.ds(g * GW, GW)
        for d in (-2, 2):
            at = 0 if d == 2 else 512
            halo_own.append(remote(keys.at[:, mine(g)], k_buf.at[at : at + 128, c], halo_dev(d)))
            halo_own.append(remote(values.at[:, mine(g)], v_buf.at[at : at + 128, c], halo_dev(d)))
    for cp in halo_own:
        cp.start()

    for cp in zb:
        cp.wait_recv()
    for i in range(16):
        rows = w_small[i].astype(F32)
        for ct in range(6):
            w_tmp[6 * i : 6 * i + 8, ct * 128 : ct * 128 + 128] = rows[ct * 8 : ct * 8 + 8, :]
    me = pl.ds(pl.multiple_of(f * FR, FR), FR)
    w_full[me, :] = w_tmp[0:FR, :].astype(BF16)

    def frame_rows(xl, yy, cc):
        return w_full.at[pl.ds(pl.multiple_of((xl * 8 + yy * 2 + cc) * FR, FR), FR)]

    chunk = frame_rows(x_lo, y, core)
    cx = remote(chunk, chunk, xlo_dev)
    cx.start()
    dy, e_cps = [], []
    for d in range(1, 4):
        dy.append(remote(chunk, chunk, y_dev(d)))
        dy[-1].start()
    e_cps.append(remote(chunk, chunk, core_dev))
    e_cps[-1].start()

    halo_par = []

    def pass_on(g):
        c = pl.ds(g * GW, GW)
        kx[g].wait_recv()
        vx[g].wait_recv()
        for d in (-2, 2):
            at = 128 if d == 2 else 640
            for buf in (k_buf, v_buf):
                halo_par.append(remote(buf.at[384:512, c], buf.at[at : at + 128, c], halo_dev(d)))
                halo_par[-1].start()

    pass_on(0)
    cx.wait_recv()
    chunk2 = frame_rows(1 - x_lo, y, core)
    for d in range(1, 4):
        dy.append(remote(chunk2, chunk2, y_dev(d)))
        dy[-1].start()
    e_cps.append(remote(chunk2, chunk2, core_dev))
    e_cps[-1].start()
    pass_on(1)
    pass_on(2)

    win_cp.wait_recv()
    for half in range(2):
        lo = win[half, 0, 0:1, :]
        hi = win[half, 1, 0:1, :]
        for j in range(6):
            base = p if j % 2 == 0 else p + 1 - 2 * s
            blk = base + 2 * (j // 2 - 1)
            ok = jnp.logical_and(lo <= blk, blk < hi)
            bias = jnp.where(ok, 0.0, -1e30).astype(F32)
            mask[half * 128 : half * 128 + 128, j * 128 : j * 128 + 128] = jnp.broadcast_to(bias, (128, 128))

    for i, cp in enumerate(dy):
        cp.wait_recv()
        d = i % 3 + 1
        got = frame_rows(x_lo if i < 3 else 1 - x_lo, lax.rem(y + 4 - d, 4), core)
        e_cps.append(remote(got, got, core_dev))
        e_cps[-1].start()

    for cp in local:
        cp.wait()
    vid_cp.wait_recv()
    for i in range(0, D, 256):
        vid_t[i : i + 256, :] = vid[:, i : i + 256].T
    for cp in e_cps:
        cp.wait_recv()

    att_cps, gh_cps, xr_cps = [], [], []

    def attention(g):
        c0 = g * GW
        q_buf[:, c0 : c0 + GW] = dot(vid[...], w_full[:, c0 : c0 + GW], 1, 0).astype(BF16)
        for cp in halo_own[4 * g : 4 * g + 4] + halo_par[4 * g : 4 * g + 4]:
            cp.wait_recv()
        dx[g].wait_recv()

        def one(hh, carry):
            c = pl.ds(pl.multiple_of(c0 + hh * HD, 128), HD)
            q = q_buf[:, c]
            k = k_buf[:, c]
            v = v_buf[:, c]
            do = do_buf[:, c]
            sc = dot(q, k, 1, 1) * SCALE + mask[...]
            top = jnp.max(sc, axis=-1, keepdims=True)
            e = jnp.exp(sc - top)
            prob = e * (1.0 / jnp.sum(e, axis=-1, keepdims=True))
            half = prob.astype(BF16)
            att_buf[:, c] = dot(half, v, 1, 0).astype(BF16)
            pg = dot(do, v, 1, 1)
            delta = jnp.sum(prob * pg, axis=-1, keepdims=True)
            ds = (prob * (pg - delta) * SCALE).astype(BF16)
            qg_buf[:, c] = dot(ds, k, 1, 0).astype(BF16)
            gk = dot(ds, q, 0, 0)
            gv = dot(half, do, 0, 0)
            for i, gr in enumerate((gk, gv)):
                gh_send[0, i, :, c] = gr[0:256].astype(BF16)
                g_mid[i, :, c] = gr[256:512]
                gh_send[1, i, :, c] = gr[512:768].astype(BF16)
            return carry

        lax.fori_loop(0, GW // HD, one, 0)
        c = pl.ds(c0, GW)
        for i, d in enumerate((-2, 2)):
            gh_cps.append(remote(gh_send.at[i, :, :, c], gh_recv.at[i, :, :, c], halo_dev(d)))
            gh_cps[-1].start()
        att_cps.append(remote(att_buf.at[ROWS : 2 * ROWS, c], att_out.at[:, mine(g)], partner))
        att_cps[-1].start()
        att_out[:, mine(g)] = att_buf[0:ROWS, c0 : c0 + GW]

    ecs, dcs, ccs, bcs, acs = [], [], [], [], []

    def weight_term(g):
        c0 = g * GW
        for i in range(0, 16, 4):
            r = dot(vid_t[i * FR : (i + 4) * FR, :], qg_buf[:, c0 : c0 + GW], 1, 0)
            for j in range(4):
                fr = i + j
                wgp[g, fr % 2, (fr // 2 % 4) * 2 + fr // 8] = r[j * FR : (j + 1) * FR]
        ecs.append(remote(wgp.at[g, 1 - core], e_recv.at[g], core_dev))
        ecs[g].start()

    def halo_back(g):
        c0 = g * GW
        for cp in gh_cps[2 * g : 2 * g + 2]:
            cp.wait_recv()
        for i, out in enumerate((gk_out, gv_out)):
            tot = g_mid[i, :, c0 : c0 + GW]
            tot = tot + gh_recv[0, i, :, c0 : c0 + GW].astype(F32) + gh_recv[1, i, :, c0 : c0 + GW].astype(F32)
            out[:, mine(g)] = tot[0:ROWS]
            x_send[i, :, c0 : c0 + GW] = tot[ROWS:].astype(BF16)
        c = pl.ds(c0, GW)
        xr_cps.append(remote(x_send.at[:, :, c], x_recv.at[:, :, c], partner))
        xr_cps[-1].start()

    def stage_d(g):
        ecs[g].wait_recv()
        for i in range(8):
            t = wgp[g, core, i] + e_recv[g, i]
            d_own[g, i] = t
            d_send[g, i] = t.astype(BF16)
        cps = []
        for d in range(1, 4):
            cps.append(remote(d_send.at[g, pl.ds(y_of(d) * 2, 2)], d_recv.at[g, d - 1], y_dev(d)))
            cps[-1].start()
        dcs.append(cps)

    def stage_c(g):
        for cp in dcs[g]:
            cp.wait_recv()
        for xl in range(2):
            t = d_own[g, y * 2 + xl]
            for d in range(3):
                t = t + d_recv[g, d, xl].astype(F32)
            c_part[g, xl] = t
        ccs.append(remote(c_part.at[g, 1 - x_lo], c_recv.at[g], xlo_dev))
        ccs[g].start()

    def stage_b(g):
        ccs[g].wait_recv()
        b_tmp[g, 0:FR, :] = c_part[g, x_lo] + c_recv[g]
        for i in range(16):
            b_part[g, i] = b_tmp[g, 6 * i : 6 * i + 8, :]
        cps = []
        for d in range(1, 8):
            cps.append(remote(b_part.at[g, pl.ds(lax.rem(z + d, 8) * 2, 2)], b_recv.at[g, d - 1], z_dev(d)))
            cps[-1].start()
        bcs.append(cps)

    def stage_a(g):
        for cp in bcs[g]:
            cp.wait_recv()
        t = b_part[g, pl.ds(z * 2, 2)]
        for d in range(7):
            t = t + b_recv[g, d]
        a_part[g] = t
        acs.append(remote(a_part.at[g, 1 - s], a_recv.at[g], partner))
        acs[g].start()
        wg_out[:, mine(g)] = a_part[g, s][0:6]

    b_tmp[...] = jnp.zeros_like(b_tmp)
    for g in range(NG):
        attention(g)
        weight_term(g)
        if g > 0:
            halo_back(g - 1)
            stage_d(g - 1)
        if g > 1:
            stage_c(g - 2)

    for i in range(0, D, 512):
        gv_send[:, i : i + 512] = dot(qg_buf[ROWS:, :], w_full[i : i + 512, :], 1, 1).astype(BF16)
    gvc = remote(gv_send, gv_recv, partner)
    gvc.start()
    halo_back(2)
    stage_d(2)
    stage_c(1)
    stage_b(0)
    for i in range(0, D, 512):
        gv_own[:, i : i + 512] = dot(qg_buf[0:ROWS, :], w_full[i : i + 512, :], 1, 1)
    stage_c(2)
    stage_b(1)
    stage_a(0)
    stage_b(2)
    stage_a(1)
    stage_a(2)

    for g in range(NG):
        xr_cps[g].wait_recv()
        c0 = g * GW
        for i, out in enumerate((gk_out, gv_out)):
            out[:, theirs(g)] = x_recv[i, :, c0 : c0 + GW].astype(F32)
    gvc.wait_recv()
    gvid_out[...] = (gv_own[...] + gv_recv[...].astype(F32)).astype(BF16)
    for g in range(NG):
        acs[g].wait_recv()
        wg_out[:, theirs(g)] = a_recv[g][0:6]
        att_cps[g].wait_recv()
    for cp in sent:
        cp.wait_send()
    assert count[0] <= NSEM


def shards(video, audio_keys, audio_values, query_weight, d_out, win_start, win_count):
    V = pltpu.VMEM
    sem = pltpu.SemaphoreType.DMA
    scratch = [
        sem((NSEM,)), sem((NSEM,)), sem((8,)),
        V((2, 2, 8, 128), jnp.int32),
        V((8, D), F32),
        V((2, 48, 128), BF16),
        V((16, 48, 128), BF16),
        V((D, HALF), BF16),
        V((104, HALF), F32),
        V((256, D), BF16),
        V((D, 256), BF16),
        V((768, HALF), BF16),
        V((768, HALF), BF16),
        V((256, HALF), BF16),
        V((256, HALF), BF16),
        V((256, 768), F32),
        V((256, HALF), BF16),
        V((256, HALF), BF16),
        V((2, 2, 256, HALF), BF16),
        V((2, 2, 256, HALF), BF16),
        V((2, 256, HALF), F32),
        V((2, ROWS, HALF), BF16),
        V((2, ROWS, HALF), BF16),
        V((ROWS, D), BF16),
        V((ROWS, D), BF16),
        V((ROWS, D), F32),
        V((NG, 2, 8, FR, GW), F32),
        V((NG, 8, FR, GW), F32),
        V((NG, 8, FR, GW), F32),
        V((NG, 8, FR, GW), BF16),
        V((NG, 3, 2, FR, GW), BF16),
        V((NG, 2, FR, GW), F32),
        V((NG, FR, GW), F32),
        V((NG, 104, GW), F32),
        V((NG, 16, 8, GW), F32),
        V((NG, 7, 2, 8, GW), F32),
        V((NG, 2, 8, GW), F32),
        V((NG, 8, GW), F32),
    ]
    hbm = pl.BlockSpec(memory_space=pl.ANY)
    vmem = pl.BlockSpec(memory_space=pltpu.VMEM)
    smem = pl.BlockSpec(memory_space=pltpu.SMEM)
    return pl.pallas_call(
        kernel,
        out_shape=(
            jax.ShapeDtypeStruct((ROWS, D), BF16),
            jax.ShapeDtypeStruct((ROWS, D), BF16),
            jax.ShapeDtypeStruct((6, D), F32),
            jax.ShapeDtypeStruct((ROWS, D), F32),
            jax.ShapeDtypeStruct((ROWS, D), F32),
        ),
        in_specs=[smem, smem, hbm, hbm, hbm, hbm, vmem],
        out_specs=(vmem,) * 5,
        scratch_shapes=scratch,
        compiler_params=pltpu.CompilerParams(
            collective_id=0, has_side_effects=True, vmem_limit_bytes=60 << 20
        ),
        cost_estimate=pl.CostEstimate(flops=4_000_000_000, bytes_accessed=8_000_000, transcendentals=1_200_000),
        name="joint",
    )(win_start, win_count, video, audio_keys, audio_values, d_out, query_weight)


def solution(mesh):
    spec = P(("frame", "head"), None)
    vec = P(("frame", "head"))
    return jax.shard_map(
        shards,
        mesh=mesh,
        in_specs=(spec, spec, spec, spec, spec, vec, vec),
        out_specs=(spec,) * 5,
        check_vma=False,
    )
```

```python
import math

import jax
import jax.numpy as jnp
from jax import lax
from jax.experimental import pallas as pl
from jax.experimental.pallas import tpu as pltpu
from jax.sharding import PartitionSpec as P

MESH = pl.DeviceIdType.MESH
HD = 128
D = 1536
HALF = 768
ROWS = 128
NG = 3
GW = HALF // NG
FR = 96
SCALE = 1.0 / math.sqrt(HD)
F32 = jnp.float32
BF16 = jnp.bfloat16
NSEM = 160


def dot(a, b, ca, cb):
    return lax.dot_general(a, b, (((ca,), (cb,)), ((), ())), preferred_element_type=F32)


def kernel(
    ws_ref, wc_ref, video, keys, values, d_out, w_ref,
    att_out, gvid_out, wg_out, gk_out, gv_out,
    ssem, rsem, lsem,
    win, wf, w_send, w4, w_pack, wz, w_tmp, w_full,
    vid, vid_t, k_buf, v_buf, do_buf, q_buf, mask, att_buf, qg_buf,
    gh_send, gh_recv, g_mid, x_send, x_recv, gv_send, gv_recv, gv_own,
    wgp, e_recv, d_send, d_recv, b_tmp, b_part, b_send, b_recv, a_tmp, a_part, a_recv,
):
    f = lax.axis_index("frame")
    h = lax.axis_index("head")
    s = lax.rem(h, 2)
    z = h // 2
    x_lo = f // 8
    y = lax.rem(f // 2, 4)
    core = lax.rem(f, 2)
    p = f * 16 + h

    partner = (f, z * 2 + 1 - s)

    def z_dev(d):
        return (f, lax.rem(z + d, 8) * 2 + s)

    def y_of(d):
        return lax.rem(y + d, 4)

    def y_dev(d):
        return (x_lo * 8 + y_of(d) * 2 + core, h)

    xlo_dev = ((1 - x_lo) * 8 + y * 2 + core, h)
    diag_dev = ((1 - x_lo) * 8 + y * 2 + core, z * 2 + 1 - s)
    core_dev = (x_lo * 8 + y * 2 + 1 - core, h)

    def halo_dev(d):
        q = lax.rem(p + d + 256, 256)
        return (q // 16, lax.rem(q, 16))

    def mine(g):
        return pl.ds(pl.multiple_of(s * HALF + g * GW, 128), GW)

    def theirs(g):
        return pl.ds(pl.multiple_of((1 - s) * HALF + g * GW, 128), GW)

    count = [0]
    sent = []

    def remote(src, dst, dev):
        i = count[0]
        count[0] += 1
        cp = pltpu.make_async_remote_copy(
            src_ref=src, dst_ref=dst, send_sem=ssem.at[i], recv_sem=rsem.at[i],
            device_id=dev, device_id_type=MESH,
        )
        sent.append(cp)
        return cp

    local = [
        pltpu.make_async_copy(video, vid.at[0:ROWS], lsem.at[0]),
        pltpu.make_async_copy(keys.at[:, pl.ds(pl.multiple_of(s * HALF, 128), HALF)], k_buf.at[256:384], lsem.at[1]),
        pltpu.make_async_copy(values.at[:, pl.ds(pl.multiple_of(s * HALF, 128), HALF)], v_buf.at[256:384], lsem.at[2]),
        pltpu.make_async_copy(d_out.at[:, pl.ds(pl.multiple_of(s * HALF, 128), HALF)], do_buf.at[0:ROWS], lsem.at[3]),
    ]
    for cp in local:
        cp.start()

    barrier = pltpu.get_barrier_semaphore()
    peers = [partner] + [z_dev(d) for d in range(1, 8)] + [y_dev(d) for d in range(1, 4)]
    peers += [xlo_dev, diag_dev, core_dev, halo_dev(-2), halo_dev(2)]
    for dev in peers:
        pl.semaphore_signal(barrier, inc=1, device_id=dev, device_id_type=MESH)

    win[0, 0] = jnp.full((8, 128), ws_ref[0], jnp.int32)
    win[0, 1] = jnp.full((8, 128), ws_ref[0] + wc_ref[0], jnp.int32)
    wf[...] = jnp.zeros_like(wf)
    wf[0:6, :] = w_ref[...].astype(F32)
    for k in range(2):
        for ct in range(0, 6, 2):
            col = k * HALF + ct * 128
            pair = jnp.concatenate([wf[:, col : col + 128], wf[:, col + 128 : col + 256]], axis=0)
            w_send[k, ct * 8 : ct * 8 + 16, :] = pair.astype(BF16)

    pl.semaphore_wait(barrier, len(peers))

    here = x_lo * 2 + s
    wa = [
        remote(w_send.at[1 - s], w4.at[here], partner),
        remote(w_send.at[s], w4.at[here], xlo_dev),
        remote(w_send.at[1 - s], w4.at[here], diag_dev),
    ]
    for cp in wa:
        cp.start()
    wl = pltpu.make_async_copy(w_send.at[s], w4.at[here], lsem.at[4])
    wl.start()
    win_cp = remote(win.at[0], win.at[1], partner)
    win_cp.start()
    kx, vx, dx = [], [], []
    for g in range(NG):
        c = pl.ds(g * GW, GW)
        kx.append(remote(keys.at[:, theirs(g)], k_buf.at[384:512, c], partner))
        vx.append(remote(values.at[:, theirs(g)], v_buf.at[384:512, c], partner))
        dx.append(remote(d_out.at[:, theirs(g)], do_buf.at[ROWS : 2 * ROWS, c], partner))
    vid_cp = remote(video, vid.at[ROWS : 2 * ROWS], partner)
    for cp in (kx[0], vx[0], kx[1], vx[1], vid_cp, dx[0], kx[2], vx[2], dx[1], dx[2]):
        cp.start()

    halo_own = []
    for g in range(NG):
        c = pl.ds(g * GW, GW)
        for d in (-2, 2):
            at = 0 if d == 2 else 512
            halo_own.append(remote(keys.at[:, mine(g)], k_buf.at[at : at + 128, c], halo_dev(d)))
            halo_own.append(remote(values.at[:, mine(g)], v_buf.at[at : at + 128, c], halo_dev(d)))
    for cp in halo_own[0:4]:
        cp.start()

    wl.wait()
    for cp in wa:
        cp.wait_recv()
    parts = [w4[i].astype(F32) for i in range(4)]
    for ct in range(6):
        for i in range(4):
            w_pack[ct * 24 + i * 6 : ct * 24 + i * 6 + 8, :] = parts[i][ct * 8 : ct * 8 + 8, :]
    wz[z] = w_pack[0:144, :].astype(BF16)
    zb = []
    for d in range(1, 8):
        zb.append(remote(wz.at[z], wz.at[z], z_dev(d)))
        zb[-1].start()
    for cp in halo_own[4:]:
        cp.start()

    for cp in zb:
        cp.wait_recv()
    for i in range(8):
        w_pack[0:144, :] = wz[i].astype(F32)
        for ct in range(6):
            for xl in range(2):
                w_tmp[xl, 12 * i : 12 * i + 16, ct * 128 : ct * 128 + 128] = w_pack[ct * 24 + xl * 12 : ct * 24 + xl * 12 + 16, :]
    own = y * 2 + core
    for xl in range(2):
        w_full[xl, own] = w_tmp[xl, 0:FR, :].astype(BF16)

    dy, e_cps = [], []
    for g in range(NG):
        c = pl.ds(g * GW, GW)
        part = w_full.at[:, own, :, c]
        dy.append([remote(part, part, y_dev(d)) for d in range(1, 4)])
        e_cps.append([remote(part, part, core_dev)])
        for cp in dy[g] + e_cps[g]:
            cp.start()

    halo_par = []

    def pass_on(g):
        c = pl.ds(g * GW, GW)
        kx[g].wait_recv()
        vx[g].wait_recv()
        for d in (-2, 2):
            at = 128 if d == 2 else 640
            for buf in (k_buf, v_buf):
                halo_par.append(remote(buf.at[384:512, c], buf.at[at : at + 128, c], halo_dev(d)))
                halo_par[-1].start()

    def to_core(g):
        c = pl.ds(g * GW, GW)
        for d in range(1, 4):
            dy[g][d - 1].wait_recv()
            part = w_full.at[:, lax.rem(y + 4 - d, 4) * 2 + core, :, c]
            e_cps[g].append(remote(part, part, core_dev))
            e_cps[g][-1].start()

    pass_on(0)
    pass_on(1)

    win_cp.wait_recv()
    for half in range(2):
        lo = win[half, 0, 0:1, :]
        hi = win[half, 1, 0:1, :]
        for j in range(6):
            base = p if j % 2 == 0 else p + 1 - 2 * s
            blk = base + 2 * (j // 2 - 1)
            ok = jnp.logical_and(lo <= blk, blk < hi)
            bias = jnp.where(ok, 0.0, -1e30).astype(F32)
            mask[half * 128 : half * 128 + 128, j * 128 : j * 128 + 128] = jnp.broadcast_to(bias, (128, 128))

    to_core(0)

    for cp in local:
        cp.wait()
    vid_cp.wait_recv()
    for i in range(0, D, 256):
        vid_t[i : i + 256, :] = vid[:, i : i + 256].T

    att_cps, gh_cps, xr_cps = [], [], []

    def project(g):
        c0 = g * GW
        for cp in e_cps[g]:
            cp.wait_recv()
        w = w_full[:, :, :, c0 : c0 + GW].reshape(D, GW)
        q_buf[:, c0 : c0 + GW] = dot(vid[...], w, 1, 0).astype(BF16)
        for cp in halo_own[4 * g : 4 * g + 4] + halo_par[4 * g : 4 * g + 4]:
            cp.wait_recv()
        dx[g].wait_recv()

    def head(g, hh):
        c = pl.ds(g * GW + hh * HD, HD)
        q = q_buf[:, c]
        k = k_buf[:, c]
        v = v_buf[:, c]
        do = do_buf[:, c]
        sc = dot(q, k, 1, 1) * SCALE + mask[...]
        top = jnp.max(sc, axis=-1, keepdims=True)
        e = jnp.exp(sc - top)
        prob = e * (1.0 / jnp.sum(e, axis=-1, keepdims=True))
        half = prob.astype(BF16)
        att_buf[:, c] = dot(half, v, 1, 0).astype(BF16)
        pg = dot(do, v, 1, 1)
        delta = jnp.sum(prob * pg, axis=-1, keepdims=True)
        ds = (prob * (pg - delta) * SCALE).astype(BF16)
        qg_buf[:, c] = dot(ds, k, 1, 0).astype(BF16)
        gk = dot(ds, q, 0, 0)
        gv = dot(half, do, 0, 0)
        for i, gr in enumerate((gk, gv)):
            gh_send[0, i, :, c] = gr[0:256].astype(BF16)
            g_mid[i, :, c] = gr[256:512]
            gh_send[1, i, :, c] = gr[512:768].astype(BF16)
        for i, d in enumerate((-2, 2)):
            gh_cps.append(remote(gh_send.at[i, :, :, c], gh_recv.at[i, :, :, c], halo_dev(d)))
            gh_cps[-1].start()

    def send_group(g):
        c0 = g * GW
        c = pl.ds(c0, GW)
        att_cps.append(remote(att_buf.at[ROWS : 2 * ROWS, c], att_out.at[:, mine(g)], partner))
        att_cps[-1].start()
        att_out[:, mine(g)] = att_buf[0:ROWS, c0 : c0 + GW]

    ecs, dcs, bcs, acs = [], [], [], []

    def weight_term(g):
        c0 = g * GW
        for i in range(0, 16, 4):
            r = dot(vid_t[i * FR : (i + 4) * FR, :], qg_buf[:, c0 : c0 + GW], 1, 0)
            for j in range(4):
                fr = i + j
                wgp[g, fr % 2, (fr // 2 % 4) * 2 + fr // 8] = r[j * FR : (j + 1) * FR]
        ecs.append(remote(wgp.at[g, 1 - core], e_recv.at[g], core_dev))
        ecs[g].start()

    def halo_back(k):
        c0 = k * HD
        for cp in gh_cps[2 * k : 2 * k + 2]:
            cp.wait_recv()
        for i, out in enumerate((gk_out, gv_out)):
            tot = g_mid[i, :, c0 : c0 + HD]
            tot = tot + gh_recv[0, i, :, c0 : c0 + HD].astype(F32) + gh_recv[1, i, :, c0 : c0 + HD].astype(F32)
            out[:, pl.ds(pl.multiple_of(s * HALF + c0, 128), HD)] = tot[0:ROWS]
            x_send[i, :, c0 : c0 + HD] = tot[ROWS:].astype(BF16)
        c = pl.ds(c0, HD)
        xr_cps.append(remote(x_send.at[:, :, c], x_recv.at[:, :, c], partner))
        xr_cps[-1].start()

    def stage_d(g):
        ecs[g].wait_recv()
        for i in range(8):
            d_send[g, i] = (wgp[g, core, i] + e_recv[g, i]).astype(BF16)
        cps = []
        for d in range(1, 4):
            cps.append(remote(d_send.at[g, pl.ds(y_of(d) * 2, 2)], d_recv.at[g, d - 1], y_dev(d)))
            cps[-1].start()
        dcs.append(cps)

    def stage_b(g):
        for cp in dcs[g]:
            cp.wait_recv()
        for xl in range(2):
            t = wgp[g, core, y * 2 + xl] + e_recv[g, y * 2 + xl]
            for d in range(3):
                t = t + d_recv[g, d, xl].astype(F32)
            b_tmp[g, xl, 0:FR, :] = t
        for i in range(8):
            for ct in range(2):
                for xl in range(2):
                    at = ct * 24 + xl * 12
                    b_part[g, i, at : at + 16, :] = b_tmp[g, xl, 12 * i : 12 * i + 16, ct * 128 : ct * 128 + 128]
            b_send[g, i] = b_part[g, i, 0:48].astype(BF16)
        cps = []
        for d in range(1, 8):
            cps.append(remote(b_send.at[g, lax.rem(z + d, 8)], b_recv.at[g, d - 1], z_dev(d)))
            cps[-1].start()
        bcs.append(cps)

    def stage_a(g):
        for cp in bcs[g]:
            cp.wait_recv()
        t = b_part[g, z, 0:48]
        for d in range(7):
            t = t + b_recv[g, d].astype(F32)
        a_tmp[g, 0:48] = t
        for i in range(4):
            for ct in range(2):
                at = ct * 24 + i * 6
                a_part[g, i, :, ct * 128 : ct * 128 + 128] = a_tmp[g, at : at + 8, :]
        cps = []
        for i, (dev, shard) in enumerate((
            (partner, x_lo * 2 + 1 - s), (xlo_dev, (1 - x_lo) * 2 + s), (diag_dev, (1 - x_lo) * 2 + 1 - s),
        )):
            cps.append(remote(a_part.at[g, shard], a_recv.at[g, i], dev))
            cps[-1].start()
        acs.append(cps)

    b_tmp[...] = jnp.zeros_like(b_tmp)
    a_tmp[...] = jnp.zeros_like(a_tmp)
    project(0)
    head(0, 0)
    pass_on(2)
    to_core(1)
    head(0, 1)
    send_group(0)
    weight_term(0)
    project(1)
    head(1, 0)
    to_core(2)
    stage_d(0)
    head(1, 1)
    send_group(1)
    weight_term(1)
    halo_back(0)
    project(2)
    head(2, 0)
    stage_d(1)
    halo_back(1)
    head(2, 1)
    send_group(2)
    weight_term(2)
    stage_b(0)
    def w_rows(i):
        return w_full[i // 768, i // 96 % 8 : i // 96 % 8 + 4].reshape(384, HALF)

    gvc = []
    for i in range(0, D, 384):
        gv_send[:, i : i + 384] = dot(qg_buf[ROWS:, :], w_rows(i), 1, 1).astype(BF16)
        gvc.append(remote(gv_send.at[:, i : i + 384], gv_recv.at[:, i : i + 384], partner))
        gvc[-1].start()
    halo_back(2)
    stage_d(2)
    halo_back(3)
    stage_b(1)
    for i in range(0, D, 384):
        gv_own[:, i : i + 384] = dot(qg_buf[0:ROWS, :], w_rows(i), 1, 1)
    stage_a(0)
    halo_back(4)
    halo_back(5)
    stage_b(2)
    stage_a(1)
    stage_a(2)

    for g in range(NG):
        xr_cps[2 * g].wait_recv()
        xr_cps[2 * g + 1].wait_recv()
        c0 = g * GW
        for i, out in enumerate((gk_out, gv_out)):
            out[:, theirs(g)] = x_recv[i, :, c0 : c0 + GW].astype(F32)
    for cp in gvc:
        cp.wait_recv()
    gvid_out[...] = (gv_own[...] + gv_recv[...].astype(F32)).astype(BF16)
    for g in range(NG):
        for cp in acs[g]:
            cp.wait_recv()
        wg_out[:, mine(g)] = (a_part[g, here] + a_recv[g, 1])[0:6]
        wg_out[:, theirs(g)] = (a_recv[g, 0] + a_recv[g, 2])[0:6]
        att_cps[g].wait_recv()
    for cp in sent:
        cp.wait_send()
    assert count[0] <= NSEM


def shards(video, audio_keys, audio_values, query_weight, d_out, win_start, win_count):
    V = pltpu.VMEM
    sem = pltpu.SemaphoreType.DMA
    scratch = [
        sem((NSEM,)), sem((NSEM,)), sem((8,)),
        V((2, 2, 8, 128), jnp.int32),
        V((8, D), F32),
        V((2, 48, 128), BF16),
        V((4, 48, 128), BF16),
        V((152, 128), F32),
        V((8, 144, 128), BF16),
        V((2, 104, HALF), F32),
        V((2, 8, FR, HALF), BF16),
        V((256, D), BF16),
        V((D, 256), BF16),
        V((768, HALF), BF16),
        V((768, HALF), BF16),
        V((256, HALF), BF16),
        V((256, HALF), BF16),
        V((256, 768), F32),
        V((256, HALF), BF16),
        V((256, HALF), BF16),
        V((2, 2, 256, HALF), BF16),
        V((2, 2, 256, HALF), BF16),
        V((2, 256, HALF), F32),
        V((2, ROWS, HALF), BF16),
        V((2, ROWS, HALF), BF16),
        V((ROWS, D), BF16),
        V((ROWS, D), BF16),
        V((ROWS, D), F32),
        V((NG, 2, 8, FR, GW), F32),
        V((NG, 8, FR, GW), F32),
        V((NG, 8, FR, GW), BF16),
        V((NG, 3, 2, FR, GW), BF16),
        V((NG, 2, 104, GW), F32),
        V((NG, 8, 56, 128), F32),
        V((NG, 8, 48, 128), BF16),
        V((NG, 7, 48, 128), BF16),
        V((NG, 56, 128), F32),
        V((NG, 4, 8, GW), F32),
        V((NG, 3, 8, GW), F32),
    ]
    hbm = pl.BlockSpec(memory_space=pl.ANY)
    vmem = pl.BlockSpec(memory_space=pltpu.VMEM)
    smem = pl.BlockSpec(memory_space=pltpu.SMEM)
    return pl.pallas_call(
        kernel,
        out_shape=(
            jax.ShapeDtypeStruct((ROWS, D), BF16),
            jax.ShapeDtypeStruct((ROWS, D), BF16),
            jax.ShapeDtypeStruct((6, D), F32),
            jax.ShapeDtypeStruct((ROWS, D), F32),
            jax.ShapeDtypeStruct((ROWS, D), F32),
        ),
        in_specs=[smem, smem, hbm, hbm, hbm, hbm, vmem],
        out_specs=(vmem,) * 5,
        scratch_shapes=scratch,
        compiler_params=pltpu.CompilerParams(
            collective_id=0, has_side_effects=True, vmem_limit_bytes=60 << 20
        ),
        cost_estimate=pl.CostEstimate(flops=4_000_000_000, bytes_accessed=8_000_000, transcendentals=1_200_000),
        name="joint",
    )(win_start, win_count, video, audio_keys, audio_values, d_out, query_weight)


def solution(mesh):
    spec = P(("frame", "head"), None)
    vec = P(("frame", "head"))
    return jax.shard_map(
        shards,
        mesh=mesh,
        in_specs=(spec, spec, spec, spec, spec, vec, vec),
        out_specs=(spec,) * 5,
        check_vma=False,
    )
```

```python
import math

import jax
import jax.numpy as jnp
from jax import lax
from jax.experimental import pallas as pl
from jax.experimental.pallas import tpu as pltpu
from jax.sharding import PartitionSpec as P

MESH = pl.DeviceIdType.MESH
HD = 128
D = 1536
HALF = 768
ROWS = 128
NG = 3
GW = HALF // NG
FR = 96
SCALE = 1.0 / math.sqrt(HD)
F32 = jnp.float32
BF16 = jnp.bfloat16
NSEM = 160


OUTS = (
    ((ROWS, D), BF16),
    ((ROWS, D), BF16),
    ((6, D), F32),
    ((ROWS, D), F32),
    ((ROWS, D), F32),
)


def dot(a, b, ca, cb):
    return lax.dot_general(a, b, (((ca,), (cb,)), ((), ())), preferred_element_type=F32)


def kernel(
    ws_ref, wc_ref, video, keys, values, d_out, w_ref,
    att_out, gvid_out, wg_out, gk_out, gv_out,
    ssem, rsem, lsem,
    win, wf, w_send, w4, w_pack, wz, w_tmp, w_full,
    vid, vid_t, kv, do_buf, q_buf, mask, att_buf, qg_buf,
    gh_send, gh_recv, g_mid, x_send, x_recv, gv_send, gv_recv, gv_own,
    wgp, e_recv, d_send, d_recv, b_tmp, b_part, b_send, b_recv, a_tmp, a_part, a_recv,
):
    f = lax.axis_index("frame")
    h = lax.axis_index("head")
    s = lax.rem(h, 2)
    z = h // 2
    x_lo = f // 8
    y = lax.rem(f // 2, 4)
    core = lax.rem(f, 2)
    p = f * 16 + h

    partner = (f, z * 2 + 1 - s)

    def z_dev(d):
        return (f, lax.rem(z + d, 8) * 2 + s)

    def y_of(d):
        return lax.rem(y + d, 4)

    def y_dev(d):
        return (x_lo * 8 + y_of(d) * 2 + core, h)

    xlo_dev = ((1 - x_lo) * 8 + y * 2 + core, h)
    diag_dev = ((1 - x_lo) * 8 + y * 2 + core, z * 2 + 1 - s)
    core_dev = (x_lo * 8 + y * 2 + 1 - core, h)

    def halo_dev(d):
        q = lax.rem(p + d + 256, 256)
        return (q // 16, lax.rem(q, 16))

    def mine(g):
        return pl.ds(pl.multiple_of(s * HALF + g * GW, 128), GW)

    def theirs(g):
        return pl.ds(pl.multiple_of((1 - s) * HALF + g * GW, 128), GW)

    count = [0]
    sent = []

    def remote(src, dst, dev):
        i = count[0]
        count[0] += 1
        cp = pltpu.make_async_remote_copy(
            src_ref=src, dst_ref=dst, send_sem=ssem.at[i], recv_sem=rsem.at[i],
            device_id=dev, device_id_type=MESH,
        )
        sent.append(cp)
        return cp

    local = [
        pltpu.make_async_copy(video, vid.at[0:ROWS], lsem.at[0]),
        pltpu.make_async_copy(keys.at[:, pl.ds(pl.multiple_of(s * HALF, 128), HALF)], kv.at[0, 256:384], lsem.at[1]),
        pltpu.make_async_copy(values.at[:, pl.ds(pl.multiple_of(s * HALF, 128), HALF)], kv.at[1, 256:384], lsem.at[2]),
        pltpu.make_async_copy(d_out.at[:, pl.ds(pl.multiple_of(s * HALF, 128), HALF)], do_buf.at[0:ROWS], lsem.at[3]),
    ]
    for cp in local:
        cp.start()

    barrier = pltpu.get_barrier_semaphore()
    peers = [partner] + [z_dev(d) for d in range(1, 8)] + [y_dev(d) for d in range(1, 4)]
    peers += [xlo_dev, diag_dev, core_dev, halo_dev(-2), halo_dev(2)]
    for dev in peers:
        pl.semaphore_signal(barrier, inc=1, device_id=dev, device_id_type=MESH)

    win[0, 0] = jnp.full((8, 128), ws_ref[0], jnp.int32)
    win[0, 1] = jnp.full((8, 128), ws_ref[0] + wc_ref[0], jnp.int32)
    wf[...] = jnp.zeros_like(wf)
    wf[0:6, :] = w_ref[...].astype(F32)
    for k in range(2):
        for ct in range(0, 6, 2):
            col = k * HALF + ct * 128
            pair = jnp.concatenate([wf[:, col : col + 128], wf[:, col + 128 : col + 256]], axis=0)
            w_send[k, ct * 8 : ct * 8 + 16, :] = pair.astype(BF16)

    pl.semaphore_wait(barrier, len(peers))

    here = x_lo * 2 + s
    wa = [
        remote(w_send.at[1 - s], w4.at[here], partner),
        remote(w_send.at[s], w4.at[here], xlo_dev),
        remote(w_send.at[1 - s], w4.at[here], diag_dev),
    ]
    for cp in wa:
        cp.start()
    wl = pltpu.make_async_copy(w_send.at[s], w4.at[here], lsem.at[4])
    wl.start()
    win_cp = remote(win.at[0], win.at[1], partner)
    win_cp.start()
    kx, vx, dx = [], [], []
    for g in range(NG):
        c = pl.ds(g * GW, GW)
        kx.append(remote(keys.at[:, theirs(g)], kv.at[0, 384:512, c], partner))
        vx.append(remote(values.at[:, theirs(g)], kv.at[1, 384:512, c], partner))
        dx.append(remote(d_out.at[:, theirs(g)], do_buf.at[ROWS : 2 * ROWS, c], partner))
    vid_cp = remote(video, vid.at[ROWS : 2 * ROWS], partner)
    for cp in (kx[0], vx[0], kx[1], vx[1], vid_cp, dx[0], kx[2], vx[2], dx[1], dx[2]):
        cp.start()

    halo = [[] for _ in range(NG)]

    def halo_send(g, at):
        for d in (-2, 2):
            to = at - 256 if d == 2 else at + 256
            c = pl.ds(g * GW, GW)
            halo[g].append(remote(kv.at[:, at : at + 128, c], kv.at[:, to : to + 128, c], halo_dev(d)))
            halo[g][-1].start()

    def pass_on(g):
        kx[g].wait_recv()
        vx[g].wait_recv()
        halo_send(g, 384)

    for cp in local:
        cp.wait()
    halo_send(0, 256)

    wl.wait()
    for cp in wa:
        cp.wait_recv()
    parts = [w4[i].astype(F32) for i in range(4)]
    for ct in range(6):
        for i in range(4):
            w_pack[ct * 24 + i * 6 : ct * 24 + i * 6 + 8, :] = parts[i][ct * 8 : ct * 8 + 8, :]
    wz[z] = w_pack[0:144, :].astype(BF16)
    zb = []
    for d in range(1, 8):
        zb.append(remote(wz.at[z], wz.at[z], z_dev(d)))
        zb[-1].start()
    pass_on(0)
    halo_send(1, 256)

    for cp in zb:
        cp.wait_recv()
    for i in range(8):
        w_pack[0:144, :] = wz[i].astype(F32)
        for ct in range(6):
            for xl in range(2):
                w_tmp[xl, 12 * i : 12 * i + 16, ct * 128 : ct * 128 + 128] = w_pack[ct * 24 + xl * 12 : ct * 24 + xl * 12 + 16, :]
    own = y * 2 + core
    for xl in range(2):
        w_full[xl, own] = w_tmp[xl, 0:FR, :].astype(BF16)

    dy, e_cps = [], []
    for g in range(NG):
        c = pl.ds(g * GW, GW)
        part = w_full.at[:, own, :, c]
        dy.append([remote(part, part, y_dev(d)) for d in range(1, 4)])
        e_cps.append([remote(part, part, core_dev)])
        for cp in dy[g] + e_cps[g]:
            cp.start()

    def to_core(g):
        c = pl.ds(g * GW, GW)
        for d in range(1, 4):
            dy[g][d - 1].wait_recv()
            part = w_full.at[:, lax.rem(y + 4 - d, 4) * 2 + core, :, c]
            e_cps[g].append(remote(part, part, core_dev))
            e_cps[g][-1].start()

    pass_on(1)
    halo_send(2, 256)

    win_cp.wait_recv()
    for half in range(2):
        lo = win[half, 0, 0:1, :]
        hi = win[half, 1, 0:1, :]
        for j in range(6):
            base = p if j % 2 == 0 else p + 1 - 2 * s
            blk = base + 2 * (j // 2 - 1)
            ok = jnp.logical_and(lo <= blk, blk < hi)
            bias = jnp.where(ok, 0.0, -1e30).astype(F32)
            mask[half * 128 : half * 128 + 128, j * 128 : j * 128 + 128] = jnp.broadcast_to(bias, (128, 128))

    to_core(0)

    vid_cp.wait_recv()
    for i in range(0, D, 256):
        vid_t[i : i + 256, :] = vid[:, i : i + 256].T

    att_cps, gh_cps, xr_cps = [], [], []

    def project(g):
        c0 = g * GW
        for cp in e_cps[g]:
            cp.wait_recv()
        w = w_full[:, :, :, c0 : c0 + GW].reshape(D, GW)
        q_buf[:, c0 : c0 + GW] = dot(vid[...], w, 1, 0).astype(BF16)
        for cp in halo[g]:
            cp.wait_recv()
        dx[g].wait_recv()

    def head(g, hh):
        c = pl.ds(g * GW + hh * HD, HD)
        q = q_buf[:, c]
        k = kv[0, :, c]
        v = kv[1, :, c]
        do = do_buf[:, c]
        sc = dot(q, k, 1, 1) * SCALE + mask[...]
        top = jnp.max(sc, axis=-1, keepdims=True)
        e = jnp.exp(sc - top)
        prob = e * (1.0 / jnp.sum(e, axis=-1, keepdims=True))
        half = prob.astype(BF16)
        att_buf[:, c] = dot(half, v, 1, 0).astype(BF16)
        pg = dot(do, v, 1, 1)
        delta = jnp.sum(prob * pg, axis=-1, keepdims=True)
        ds = (prob * (pg - delta) * SCALE).astype(BF16)
        qg_buf[:, c] = dot(ds, k, 1, 0).astype(BF16)
        gk = dot(ds, q, 0, 0)
        gv = dot(half, do, 0, 0)
        for i, gr in enumerate((gk, gv)):
            gh_send[0, i, :, c] = gr[0:256].astype(BF16)
            g_mid[i, :, c] = gr[256:512]
            gh_send[1, i, :, c] = gr[512:768].astype(BF16)
        for i, d in enumerate((-2, 2)):
            gh_cps.append(remote(gh_send.at[i, :, :, c], gh_recv.at[i, :, :, c], halo_dev(d)))
            gh_cps[-1].start()

    def send_group(g):
        c0 = g * GW
        c = pl.ds(c0, GW)
        att_cps.append(remote(att_buf.at[ROWS : 2 * ROWS, c], att_out.at[:, mine(g)], partner))
        att_cps[-1].start()
        att_out[:, mine(g)] = att_buf[0:ROWS, c0 : c0 + GW]

    ecs, dcs, bcs, acs = [], [], [], []

    def weight_term(g):
        c0 = g * GW
        for i in range(0, 16, 4):
            r = dot(vid_t[i * FR : (i + 4) * FR, :], qg_buf[:, c0 : c0 + GW], 1, 0)
            for j in range(4):
                fr = i + j
                wgp[g, fr % 2, (fr // 2 % 4) * 2 + fr // 8] = r[j * FR : (j + 1) * FR]
        ecs.append(remote(wgp.at[g, 1 - core], e_recv.at[g], core_dev))
        ecs[g].start()

    def halo_back(k):
        c0 = k * HD
        for cp in gh_cps[2 * k : 2 * k + 2]:
            cp.wait_recv()
        for i, out in enumerate((gk_out, gv_out)):
            tot = g_mid[i, :, c0 : c0 + HD]
            tot = tot + gh_recv[0, i, :, c0 : c0 + HD].astype(F32) + gh_recv[1, i, :, c0 : c0 + HD].astype(F32)
            out[:, pl.ds(pl.multiple_of(s * HALF + c0, 128), HD)] = tot[0:ROWS]
            x_send[i, :, c0 : c0 + HD] = tot[ROWS:].astype(BF16)
        c = pl.ds(c0, HD)
        xr_cps.append(remote(x_send.at[:, :, c], x_recv.at[:, :, c], partner))
        xr_cps[-1].start()

    def stage_d(g):
        ecs[g].wait_recv()
        for i in range(8):
            d_send[g, i] = (wgp[g, core, i] + e_recv[g, i]).astype(BF16)
        cps = []
        for d in range(1, 4):
            cps.append(remote(d_send.at[g, pl.ds(y_of(d) * 2, 2)], d_recv.at[g, d - 1], y_dev(d)))
            cps[-1].start()
        dcs.append(cps)

    def stage_b(g):
        for cp in dcs[g]:
            cp.wait_recv()
        for xl in range(2):
            t = wgp[g, core, y * 2 + xl] + e_recv[g, y * 2 + xl]
            for d in range(3):
                t = t + d_recv[g, d, xl].astype(F32)
            b_tmp[g, xl, 0:FR, :] = t
        for i in range(8):
            for ct in range(2):
                for xl in range(2):
                    at = ct * 24 + xl * 12
                    b_part[g, i, at : at + 16, :] = b_tmp[g, xl, 12 * i : 12 * i + 16, ct * 128 : ct * 128 + 128]
            b_send[g, i] = b_part[g, i, 0:48].astype(BF16)
        cps = []
        for d in range(1, 8):
            cps.append(remote(b_send.at[g, lax.rem(z + d, 8)], b_recv.at[g, d - 1], z_dev(d)))
            cps[-1].start()
        bcs.append(cps)

    def stage_a(g):
        for cp in bcs[g]:
            cp.wait_recv()
        t = b_part[g, z, 0:48]
        for d in range(7):
            t = t + b_recv[g, d].astype(F32)
        a_tmp[g, 0:48] = t
        for i in range(4):
            for ct in range(2):
                at = ct * 24 + i * 6
                a_part[g, i, :, ct * 128 : ct * 128 + 128] = a_tmp[g, at : at + 8, :]
        cps = []
        for i, (dev, shard) in enumerate((
            (partner, x_lo * 2 + 1 - s), (xlo_dev, (1 - x_lo) * 2 + s), (diag_dev, (1 - x_lo) * 2 + 1 - s),
        )):
            cps.append(remote(a_part.at[g, shard], a_recv.at[g, i], dev))
            cps[-1].start()
        acs.append(cps)

    b_tmp[...] = jnp.zeros_like(b_tmp)
    a_tmp[...] = jnp.zeros_like(a_tmp)
    project(0)
    head(0, 0)
    to_core(1)
    head(0, 1)
    pass_on(2)
    send_group(0)
    weight_term(0)
    to_core(2)
    project(1)
    head(1, 0)
    stage_d(0)
    head(1, 1)
    send_group(1)
    weight_term(1)
    halo_back(0)
    project(2)
    head(2, 0)
    stage_d(1)
    halo_back(1)
    head(2, 1)
    send_group(2)
    weight_term(2)
    stage_b(0)
    def w_rows(i):
        return w_full[i // 768, i // 96 % 8 : i // 96 % 8 + 4].reshape(384, HALF)

    gvc = []
    for i in range(0, D, 384):
        gv_send[:, i : i + 384] = dot(qg_buf[ROWS:, :], w_rows(i), 1, 1).astype(BF16)
        gvc.append(remote(gv_send.at[:, i : i + 384], gv_recv.at[:, i : i + 384], partner))
        gvc[-1].start()
    halo_back(2)
    stage_d(2)
    halo_back(3)
    stage_b(1)
    for i in range(0, D, 384):
        gv_own[:, i : i + 384] = dot(qg_buf[0:ROWS, :], w_rows(i), 1, 1)
    stage_a(0)
    halo_back(4)
    halo_back(5)
    stage_b(2)
    stage_a(1)
    stage_a(2)

    for g in range(NG):
        xr_cps[2 * g].wait_recv()
        xr_cps[2 * g + 1].wait_recv()
        c0 = g * GW
        for i, out in enumerate((gk_out, gv_out)):
            out[:, theirs(g)] = x_recv[i, :, c0 : c0 + GW].astype(F32)
    for cp in gvc:
        cp.wait_recv()
    gvid_out[...] = (gv_own[...] + gv_recv[...].astype(F32)).astype(BF16)
    for g in range(NG):
        for cp in acs[g]:
            cp.wait_recv()
        wg_out[:, mine(g)] = (a_part[g, here] + a_recv[g, 1])[0:6]
        wg_out[:, theirs(g)] = (a_recv[g, 0] + a_recv[g, 2])[0:6]
        att_cps[g].wait_recv()
    for cp in sent:
        cp.wait_send()
    assert count[0] <= NSEM


def shards(video, audio_keys, audio_values, query_weight, d_out, win_start, win_count):
    V = pltpu.VMEM
    sem = pltpu.SemaphoreType.DMA
    scratch = [
        sem((NSEM,)), sem((NSEM,)), sem((8,)),
        V((2, 2, 8, 128), jnp.int32),
        V((8, D), F32),
        V((2, 48, 128), BF16),
        V((4, 48, 128), BF16),
        V((152, 128), F32),
        V((8, 144, 128), BF16),
        V((2, 104, HALF), F32),
        V((2, 8, FR, HALF), BF16),
        V((256, D), BF16),
        V((D, 256), BF16),
        V((2, 768, HALF), BF16),
        V((256, HALF), BF16),
        V((256, HALF), BF16),
        V((256, 768), F32),
        V((256, HALF), BF16),
        V((256, HALF), BF16),
        V((2, 2, 256, HALF), BF16),
        V((2, 2, 256, HALF), BF16),
        V((2, 256, HALF), F32),
        V((2, ROWS, HALF), BF16),
        V((2, ROWS, HALF), BF16),
        V((ROWS, D), BF16),
        V((ROWS, D), BF16),
        V((ROWS, D), F32),
        V((NG, 2, 8, FR, GW), F32),
        V((NG, 8, FR, GW), F32),
        V((NG, 8, FR, GW), BF16),
        V((NG, 3, 2, FR, GW), BF16),
        V((NG, 2, 104, GW), F32),
        V((NG, 8, 56, 128), F32),
        V((NG, 8, 48, 128), BF16),
        V((NG, 7, 48, 128), BF16),
        V((NG, 56, 128), F32),
        V((NG, 4, 8, GW), F32),
        V((NG, 3, 8, GW), F32),
    ]
    hbm = pl.BlockSpec(memory_space=pl.ANY)
    vmem = pl.BlockSpec(memory_space=pltpu.VMEM)
    smem = pl.BlockSpec(memory_space=pltpu.SMEM)
    outs = pl.pallas_call(
        kernel,
        out_shape=tuple(V(shape, kind) for shape, kind in OUTS),
        in_specs=[smem, smem, hbm, hbm, hbm, hbm, vmem],
        out_specs=(vmem,) * 5,
        scratch_shapes=scratch,
        compiler_params=pltpu.CompilerParams(
            collective_id=0, has_side_effects=True, vmem_limit_bytes=60 << 20
        ),
        cost_estimate=pl.CostEstimate(flops=4_000_000_000, bytes_accessed=8_000_000, transcendentals=1_200_000),
        name="joint",
    )(win_start, win_count, video, audio_keys, audio_values, d_out, query_weight)
    return outs


def solution(mesh):
    spec = P(("frame", "head"), None)
    vec = P(("frame", "head"))
    return jax.shard_map(
        shards,
        mesh=mesh,
        in_specs=(spec, spec, spec, spec, spec, vec, vec),
        out_specs=(spec,) * 5,
        check_vma=False,
    )
```
